512 devices in a mesh: ctx: 16 (over z), head: 32 (over y, x, core).
Axes of the slice: x: 4, y: 4, z: 16, core: 2. Of those that a mesh axis runs over, the one named last changes fastest.
Arguments:
- queries: bfloat16 [16384, 8192], P(('ctx', 'head')), may hold values from -12 to 12
- key_state_rows: bfloat16 [16384, 1024], P(('ctx', 'head')), may hold values from -3.5 to 3.5
- value_state_rows: bfloat16 [16384, 1024], P(('ctx', 'head')), may hold values from -6 to 6
- attn_output: bfloat16 [16384, 8192], P(('ctx', 'head')), may hold values from -6 to 6
- grad_output: bfloat16 [16384, 8192], P(('ctx', 'head')), may hold values from -6 to 6
- doc_ids: int32 [16384], replicated, may hold values from 0 to 63, never falling along the last dimension, each value on 1 to 1024 neighbouring positions
Outputs:
- grad_queries: bfloat16 [16384, 8192], P(('ctx', 'head'))
- key_state_gradient: bfloat16 [16384, 1024], P(('ctx', 'head'))
- value_state_gradient: bfloat16 [16384, 1024], P(('ctx', 'head'))
The draws below stay inside these ranges and needn't reach their ends.
All inputs are finite; a program needn't handle non-finite values.
Results may differ from the reference program's by a relative error of at most 0.005.
Values may be sent and summed in bfloat16 or wider, within the bound.
No kernel may reach another device: no remote copies, remote signals or barrier semaphores. Data moves between devices by JAX's collectives and lax.ppermute only.
A program may use at most 64 MiB of HBM per device.

```python
import math
import jax
import jax.numpy as jnp
import numpy as np
from jax import lax

QUERY_HEAD_COUNT = 64
KEY_VALUE_HEADS = 8
HEAD_SIZE = 128
GROUP_TOKENS = 1024
WINDOW_TOKENS = 16384
DOCS = 64
N_CTX = 16


def draw_key_state_rows(key, part):
    key = jax.random.fold_in(key, 11)
    hidden_states = jnp.clip(jax.random.normal(key, (WINDOW_TOKENS, KEY_VALUE_HEADS * HEAD_SIZE), jnp.float32), -3.5, 3.5)
    return hidden_states.astype(jnp.bfloat16)


def draw_queries(key, part):
    key = jax.random.fold_in(key, 23)
    hidden_states = jnp.clip(jax.random.normal(key, (WINDOW_TOKENS, QUERY_HEAD_COUNT * HEAD_SIZE), jnp.float32), -4.0, 4.0)
    return hidden_states.astype(jnp.bfloat16)


def level_of(key, dims, pieces, least, high):
    def one(axis_at, shards_of):
        steps = jax.random.uniform(jax.random.fold_in(jax.random.fold_in(key, 6), axis_at), (shards_of,), jnp.float32, least / len(pieces), high / len(pieces))
        return jnp.repeat(jnp.exp(steps), dims[axis_at] // shards_of).reshape((-1,) + (1,) * (len(dims) - axis_at - 1))

    factor_of = one(*pieces[0])
    for cut in pieces[1:]:
        factor_of = factor_of * one(*cut)
    return factor_of


def split_up(number_of, total, reach, lean):
    portions = [(1 << 20) // math.isqrt(grade ** lean) + 1 for grade in range(2, number_of + 1)]
    surplus, given = total - reach - (number_of - 1), [1] * (number_of - 1)
    while surplus > 0:
        candidates = [i for i in range(number_of - 1) if given[i] < reach]
        pool, left = sum([portions[i] for i in candidates]), surplus
        for i in candidates:
            addition = min(reach - given[i], max(1, left * portions[i] // pool), surplus)
            given[i] = given[i] + addition
            surplus = surplus - addition
    return np.array([reach] + given)


def ragged(stream_key, number_of, total, most, lean):
    if number_of == 2:
        one = jax.random.randint(stream_key, (), max(1, total - most), min(most, total - 1) + 1)
        return jnp.stack([one, total - one])
    tallies = jnp.asarray(split_up(number_of, total, most, lean), jnp.int32)
    pairs = (number_of - 1) // 2
    source_of, receiver = tallies[1:1 + 2 * pairs:2], tallies[2:2 + 2 * pairs:2]
    slack = jnp.minimum(source_of - 1, most - receiver)
    passed = jax.random.randint(jax.random.fold_in(stream_key, 1), (pairs,), 0, 1 << 20) % (slack + 1)
    tallies = tallies.at[1:1 + 2 * pairs:2].set(source_of - passed).at[2:2 + 2 * pairs:2].set(receiver + passed)
    return tallies[jax.random.permutation(jax.random.fold_in(stream_key, 2), number_of)]


def normal_values(rng, shape, scale, bound, cuts=(), kind=jnp.bfloat16):
    values = scale * jax.random.normal(rng, shape, jnp.float32)
    if cuts:
        values = values * level_of(rng, shape, cuts, -0.22, 0.18)
    return jnp.clip(values, -bound, bound).astype(kind)


def setup_inputs(seed: int = 0) -> dict:
    key_of = jax.random.split(jax.random.key(seed), 7)
    return {
        "queries": draw_queries(jax.random.fold_in(key_of[6], 71), 0),
        "key_state_rows": draw_key_state_rows(jax.random.fold_in(key_of[6], 71), 0),
        "value_state_rows": normal_values(key_of[2], (WINDOW_TOKENS, KEY_VALUE_HEADS * HEAD_SIZE), 1.0, 6.0, ((0, 512),)),
        "attn_output": normal_values(key_of[3], (WINDOW_TOKENS, QUERY_HEAD_COUNT * HEAD_SIZE), 1.0, 6.0, ((0, 512),)),
        "grad_output": normal_values(key_of[4], (WINDOW_TOKENS, QUERY_HEAD_COUNT * HEAD_SIZE), 1.0, 6.0, ((0, 512),)),
        "doc_ids": jnp.searchsorted(jnp.cumsum(ragged(key_of[5], DOCS, WINDOW_TOKENS, GROUP_TOKENS, 2)), jnp.arange(WINDOW_TOKENS), side="right").astype(jnp.int32),
    }


def head_grads(query_heads, keys, values, grad_heads, row_delta, visible):
    score_scale = 1.0 / math.sqrt(HEAD_SIZE)
    seen = (visible == 1)[None]
    query_wide = query_heads.astype(jnp.float32)
    keys_wide = keys.astype(jnp.float32)
    values_wide = values.astype(jnp.float32)
    grad_wide = grad_heads.astype(jnp.float32)
    scores = jnp.einsum('rqd,kd->rqk', query_wide, keys_wide) * score_scale
    masked = jnp.where(seen, scores, -1e+30)
    largest = lax.optimization_barrier(jnp.max(masked, axis=-1, keepdims=True))
    weights = jnp.where(seen, jnp.exp(masked - largest), 0.0)
    probs = weights / lax.optimization_barrier(jnp.sum(weights, axis=-1, keepdims=True))
    probs_low = probs.astype(jnp.bfloat16)
    grad_value = jnp.einsum('rqk,rqd->kd', probs_low.astype(jnp.float32), grad_wide)
    grad_probs = jnp.einsum('rqd,kd->rqk', grad_wide, values_wide)
    grad_scores = (probs * (grad_probs - row_delta[..., None])).astype(jnp.bfloat16)
    scores_wide = grad_scores.astype(jnp.float32)
    grad_query = jnp.einsum('rqk,kd->rqd', scores_wide, keys_wide) * score_scale
    grad_key = jnp.einsum('rqk,rqd->kd', scores_wide, query_wide) * score_scale
    return (grad_query, grad_key, grad_value)

def reference(queries, key_state_rows, value_state_rows, attn_output, grad_output, doc_ids):
    query_group_ratio = QUERY_HEAD_COUNT // KEY_VALUE_HEADS
    key_padding = jnp.concatenate([jnp.zeros((GROUP_TOKENS, KEY_VALUE_HEADS * HEAD_SIZE), jnp.bfloat16), key_state_rows], axis=0)
    value_padding = jnp.concatenate([jnp.zeros((GROUP_TOKENS, KEY_VALUE_HEADS * HEAD_SIZE), jnp.bfloat16), value_state_rows], axis=0)
    seg_pad = jnp.concatenate([jnp.full((GROUP_TOKENS,), -1, jnp.int32), doc_ids.astype(jnp.int32)], axis=0)

    def one_group(group_index):
        start_offset = (group_index * GROUP_TOKENS).astype(jnp.int32)
        query_block = lax.dynamic_slice_in_dim(queries, start_offset, GROUP_TOKENS, 0).reshape(GROUP_TOKENS, QUERY_HEAD_COUNT, HEAD_SIZE)
        out_block = lax.dynamic_slice_in_dim(attn_output, start_offset, GROUP_TOKENS, 0).reshape(GROUP_TOKENS, QUERY_HEAD_COUNT, HEAD_SIZE)
        grad_block = lax.dynamic_slice_in_dim(grad_output, start_offset, GROUP_TOKENS, 0).reshape(GROUP_TOKENS, QUERY_HEAD_COUNT, HEAD_SIZE)
        key_tile_block = lax.dynamic_slice_in_dim(key_padding, start_offset, 2 * GROUP_TOKENS, 0).reshape(2 * GROUP_TOKENS, KEY_VALUE_HEADS, HEAD_SIZE)
        value_tile_block = lax.dynamic_slice_in_dim(value_padding, start_offset, 2 * GROUP_TOKENS, 0).reshape(2 * GROUP_TOKENS, KEY_VALUE_HEADS, HEAD_SIZE)
        seg_query = lax.dynamic_slice_in_dim(doc_ids.astype(jnp.int32), start_offset, GROUP_TOKENS, 0)
        seg_key = lax.dynamic_slice_in_dim(seg_pad, start_offset, 2 * GROUP_TOKENS, 0)
        pos_query = jnp.arange(GROUP_TOKENS, dtype=jnp.int32) + GROUP_TOKENS
        pos_key = jnp.arange(2 * GROUP_TOKENS, dtype=jnp.int32)
        visible = jnp.where((seg_key[None, :] == seg_query[:, None]) & (pos_key[None, :] <= pos_query[:, None]), 1, 0).astype(jnp.int32)
        delta_all = lax.optimization_barrier(jnp.sum(grad_block.astype(jnp.float32) * out_block.astype(jnp.float32), axis=-1))
        query_parts, key_parts, value_parts = ([], [], [])
        for shared_value_head in range(KEY_VALUE_HEADS):
            first = shared_value_head * query_group_ratio
            query_heads = jnp.transpose(query_block[:, first:first + query_group_ratio, :], (1, 0, 2))
            grad_heads = jnp.transpose(grad_block[:, first:first + query_group_ratio, :], (1, 0, 2))
            row_delta = jnp.transpose(delta_all[:, first:first + query_group_ratio], (1, 0))
            grad_query, grad_key, grad_value = head_grads(query_heads, key_tile_block[:, shared_value_head, :], value_tile_block[:, shared_value_head, :], grad_heads, row_delta, visible)
            query_parts.append(jnp.transpose(grad_query, (1, 0, 2)))
            key_parts.append(grad_key)
            value_parts.append(grad_value)
        grad_q_block = jnp.concatenate(query_parts, axis=1).reshape(GROUP_TOKENS, QUERY_HEAD_COUNT * HEAD_SIZE).astype(jnp.bfloat16)
        return (grad_q_block, jnp.concatenate(key_parts, axis=1), jnp.concatenate(value_parts, axis=1))
    grad_q_groups, key_groups, value_groups = lax.map(one_group, jnp.arange(N_CTX, dtype=jnp.int32))
    trailing_zero_rows = jnp.zeros((1, GROUP_TOKENS, KEY_VALUE_HEADS * HEAD_SIZE), jnp.float32)
    key_grand_total = key_groups[:, GROUP_TOKENS:] + jnp.concatenate([key_groups[1:, :GROUP_TOKENS], trailing_zero_rows], axis=0)
    value_grand_total = value_groups[:, GROUP_TOKENS:] + jnp.concatenate([value_groups[1:, :GROUP_TOKENS], trailing_zero_rows], axis=0)
    grad_queries = grad_q_groups.reshape(WINDOW_TOKENS, QUERY_HEAD_COUNT * HEAD_SIZE)
    key_state_gradient = key_grand_total.reshape(WINDOW_TOKENS, KEY_VALUE_HEADS * HEAD_SIZE).astype(jnp.bfloat16)
    value_state_gradient = value_grand_total.reshape(WINDOW_TOKENS, KEY_VALUE_HEADS * HEAD_SIZE).astype(jnp.bfloat16)
    return (grad_queries, key_state_gradient, value_state_gradient)
```

```python
import math

import jax
import jax.numpy as jnp
from jax import lax
from jax.experimental import pallas as pl
from jax.experimental.pallas import tpu as pltpu
from jax.sharding import PartitionSpec as P

QUERY_HEAD_COUNT = 64
KEY_VALUE_HEADS = 8
HEAD_SIZE = 128
HEADS_EACH = QUERY_HEAD_COUNT // KEY_VALUE_HEADS
COLUMNS = HEADS_EACH * HEAD_SIZE
BEHIND = 4
SCALE = 1.0 / math.sqrt(HEAD_SIZE)
LOG2E = math.log2(math.e)
VMEM = pl.BlockSpec(memory_space=pltpu.VMEM)


def params(megabytes):
    return pltpu.CompilerParams(vmem_limit_bytes=megabytes * 1024 * 1024)


def contract_last(left, right):
    return lax.dot_general(
        left, right, (((1,), (1,)), ((), ())), preferred_element_type=jnp.float32
    )


def pack_keys_kernel(key_ref, value_ref, out_ref):
    for c in range(KEY_VALUE_HEADS):
        columns = slice(c * HEAD_SIZE, (c + 1) * HEAD_SIZE)
        out_ref[c, :, :HEAD_SIZE] = key_ref[:, columns]
        out_ref[c, :, HEAD_SIZE:] = value_ref[:, columns]


def pack_keys(keys, values):
    rows = keys.shape[0]
    return pl.pallas_call(
        pack_keys_kernel,
        out_shape=jax.ShapeDtypeStruct((KEY_VALUE_HEADS, rows, 2 * HEAD_SIZE), jnp.bfloat16),
        in_specs=[VMEM] * 2,
        out_specs=VMEM,
        name="pack_keys",
    )(keys, values)


def pack_queries_kernel(query_ref, out_ref, grad_ref, packed_ref):
    rows = query_ref.shape[0]
    lane = lax.broadcasted_iota(jnp.int32, (rows, HEAD_SIZE), 1)
    for c in range(KEY_VALUE_HEADS):
        columns = slice(c * COLUMNS, (c + 1) * COLUMNS)
        packed_ref[c, :, :COLUMNS] = query_ref[:, columns]
        packed_ref[c, :, COLUMNS : 2 * COLUMNS] = grad_ref[:, columns]
        terms = jnp.zeros((rows, HEAD_SIZE), jnp.float32)
        for h in range(HEADS_EACH):
            head = slice(c * COLUMNS + h * HEAD_SIZE, c * COLUMNS + (h + 1) * HEAD_SIZE)
            delta = jnp.sum(
                grad_ref[:, head].astype(jnp.float32) * out_ref[:, head].astype(jnp.float32),
                axis=-1,
                keepdims=True,
            )
            high = delta.astype(jnp.bfloat16).astype(jnp.float32)
            rest = delta - high
            middle = rest.astype(jnp.bfloat16).astype(jnp.float32)
            terms = jnp.where(lane == h, high, terms)
            terms = jnp.where(lane == HEADS_EACH + h, middle, terms)
            terms = jnp.where(lane == 2 * HEADS_EACH + h, rest - middle, terms)
        packed_ref[c, :, 2 * COLUMNS :] = terms.astype(jnp.bfloat16)


def pack_queries(queries, outputs, grads):
    rows = queries.shape[0]
    return pl.pallas_call(
        pack_queries_kernel,
        out_shape=jax.ShapeDtypeStruct(
            (KEY_VALUE_HEADS, rows, 2 * COLUMNS + HEAD_SIZE), jnp.bfloat16
        ),
        in_specs=[VMEM] * 3,
        out_specs=VMEM,
        name="pack_queries",
    )(queries, outputs, grads)


def attend_kernel(
    packed_ref, kv0, kv1, kv2, kv3, kv4, first_ref,
    grad_query_ref, out0, out1, out2, out3, out4,
    bias, key_turned, scores, delta, key_total, value_total,
):
    kv = (kv0, kv1, kv2, kv3, kv4)
    outs = (out0, out1, out2, out3, out4)
    block = kv0.shape[0]
    parts = len(kv)
    rows = [slice(j * block, (j + 1) * block) for j in range(parts)]
    first = first_ref[...]
    last = lax.broadcasted_iota(jnp.int32, (1, block), 1) + (parts - 1) * block
    for j in range(parts):
        key_at = lax.broadcasted_iota(jnp.int32, (block, block), 0) + j * block
        seen = (key_at >= first) & (key_at <= last)
        bias[rows[j], :] = jnp.where(seen, 0.0, -1e30)
        key_turned[:, rows[j]] = kv[j][:, :HEAD_SIZE].astype(jnp.float32).T.astype(jnp.bfloat16)
    terms = packed_ref[:, 2 * COLUMNS :].astype(jnp.float32).T
    delta[...] = (
        terms[:HEADS_EACH] + terms[HEADS_EACH : 2 * HEADS_EACH]
        + terms[2 * HEADS_EACH : 3 * HEADS_EACH]
    )
    key_total[...] = jnp.zeros_like(key_total)
    value_total[...] = jnp.zeros_like(value_total)

    def one_head(h, carry):
        at = pl.multiple_of(h * HEAD_SIZE, HEAD_SIZE)
        query = packed_ref[:, pl.ds(at, HEAD_SIZE)]
        grad = packed_ref[:, pl.ds(COLUMNS + at, HEAD_SIZE)]
        row_delta = delta[pl.ds(h, 1), :]
        largest = jnp.full((1, block), -jnp.inf, jnp.float32)
        for j in range(parts):
            part = contract_last(kv[j][:, :HEAD_SIZE], query) * (SCALE * LOG2E) + bias[rows[j], :]
            scores[rows[j], :] = part
            largest = jnp.maximum(largest, jnp.max(part, axis=0, keepdims=True))
        total = jnp.zeros((1, block), jnp.float32)
        for j in range(parts):
            part = jnp.exp2(scores[rows[j], :] - largest)
            scores[rows[j], :] = part
            total = total + jnp.sum(part, axis=0, keepdims=True)
        inverse = 1.0 / total
        query_grad = jnp.zeros((HEAD_SIZE, block), jnp.float32)
        for j in range(parts):
            probs = scores[rows[j], :] * inverse
            value_total[rows[j], :] += jnp.dot(
                probs.astype(jnp.bfloat16), grad, preferred_element_type=jnp.float32
            )
            grad_probs = contract_last(kv[j][:, HEAD_SIZE:], grad)
            grad_scores = (probs * (grad_probs - row_delta)).astype(jnp.bfloat16)
            key_total[rows[j], :] += jnp.dot(
                grad_scores, query, preferred_element_type=jnp.float32
            )
            query_grad = query_grad + jnp.dot(
                key_turned[:, rows[j]], grad_scores, preferred_element_type=jnp.float32
            )
        grad_query_ref[:, pl.ds(at, HEAD_SIZE)] = (query_grad * SCALE).T.astype(jnp.bfloat16)
        return carry

    lax.fori_loop(0, HEADS_EACH, one_head, 0)
    for j in range(parts):
        outs[j][:, :HEAD_SIZE] = (key_total[rows[j], :] * SCALE).astype(outs[j].dtype)
        outs[j][:, HEAD_SIZE:] = value_total[rows[j], :].astype(outs[j].dtype)


def attend(packed, kv, first):
    block = packed.shape[0]
    keys = block * len(kv)
    part = (block, 2 * HEAD_SIZE)
    return pl.pallas_call(
        attend_kernel,
        out_shape=[jax.ShapeDtypeStruct((block, COLUMNS), jnp.bfloat16)]
        + [jax.ShapeDtypeStruct(part, jnp.bfloat16)] * BEHIND
        + [jax.ShapeDtypeStruct(part, jnp.float32)],
        in_specs=[VMEM] * (2 + len(kv)),
        out_specs=[VMEM] * (1 + len(kv)),
        scratch_shapes=[
            pltpu.VMEM((keys, block), jnp.float32),
            pltpu.VMEM((HEAD_SIZE, keys), jnp.bfloat16),
            pltpu.VMEM((keys, block), jnp.float32),
            pltpu.VMEM((HEADS_EACH, block), jnp.float32),
            pltpu.VMEM((keys, HEAD_SIZE), jnp.float32),
            pltpu.VMEM((keys, HEAD_SIZE), jnp.float32),
        ],
        compiler_params=params(32),
        name="attend",
    )(packed, *kv, first)


def add_kernel(own_ref, ref1, ref2, ref3, ref4, out_ref):
    total = own_ref[...]
    for ref in (ref1, ref2, ref3, ref4):
        total = total + ref[...].astype(jnp.float32)
    out_ref[...] = total.astype(jnp.bfloat16)


def add_parts(own, others):
    return pl.pallas_call(
        add_kernel,
        out_shape=jax.ShapeDtypeStruct(own.shape, jnp.bfloat16),
        in_specs=[VMEM] * (1 + len(others)),
        out_specs=VMEM,
        name="add_parts",
    )(own, *others)


def unpack_queries_kernel(in_ref, out_ref):
    for c in range(KEY_VALUE_HEADS):
        out_ref[:, c * COLUMNS : (c + 1) * COLUMNS] = in_ref[c]


def unpack_queries(packed):
    rows = packed.shape[1]
    return pl.pallas_call(
        unpack_queries_kernel,
        out_shape=jax.ShapeDtypeStruct((rows, KEY_VALUE_HEADS * COLUMNS), jnp.bfloat16),
        in_specs=[VMEM],
        out_specs=VMEM,
        name="unpack_queries",
    )(packed)


def unpack_keys_kernel(in_ref, key_ref, value_ref):
    for c in range(KEY_VALUE_HEADS):
        columns = slice(c * HEAD_SIZE, (c + 1) * HEAD_SIZE)
        key_ref[:, columns] = in_ref[c, :, :HEAD_SIZE]
        value_ref[:, columns] = in_ref[c, :, HEAD_SIZE:]


def unpack_keys(packed):
    rows = packed.shape[1]
    shape = jax.ShapeDtypeStruct((rows, KEY_VALUE_HEADS * HEAD_SIZE), jnp.bfloat16)
    return pl.pallas_call(
        unpack_keys_kernel,
        out_shape=[shape, shape],
        in_specs=[VMEM],
        out_specs=[VMEM] * 2,
        name="unpack_keys",
    )(packed)


def on_device(queries, key_state_rows, value_state_rows, attn_output, grad_output, doc_ids):
    placements = lax.axis_size("head")
    contexts = lax.axis_size("ctx")
    rows = queries.shape[0]
    sharers = KEY_VALUE_HEADS
    blocks_each = placements // sharers
    block = rows * sharers
    teams = [[t * sharers + i for i in range(sharers)] for t in range(blocks_each)]

    def exchange(value):
        return lax.all_to_all(
            value, "head", split_axis=0, concat_axis=0, axis_index_groups=teams, tiled=True
        )

    def shift(value, steps):
        count = contexts * blocks_each
        pairs = [
            (source * sharers + i, (source + steps) * sharers + i)
            for source in range(count)
            if 0 <= source + steps < count
            for i in range(sharers)
        ]
        return lax.ppermute(value, ("ctx", "head"), pairs)

    at = lax.axis_index("ctx") * blocks_each + lax.axis_index("head") // sharers
    padded = jnp.concatenate([jnp.full((BEHIND * block,), -1, jnp.int32), doc_ids])
    seg_key = lax.dynamic_slice_in_dim(padded, at * block, (BEHIND + 1) * block, 0)
    seg_query = seg_key[BEHIND * block :]
    first = jnp.sum((seg_key[:, None] < seg_query[None, :]).astype(jnp.int32), axis=0)[None, :]

    own = exchange(pack_keys(key_state_rows, value_state_rows)).reshape(block, 2 * HEAD_SIZE)
    packed = exchange(pack_queries(queries, attn_output, grad_output))
    packed = packed.reshape(block, 2 * COLUMNS + HEAD_SIZE)
    kv = [shift(own, steps) for steps in range(BEHIND, 0, -1)] + [own]
    grad_query, *grad_kv = attend(packed, kv, first)
    grad_rows = exchange(grad_query.reshape(sharers, rows, COLUMNS))
    others = [shift(grad_kv[j], j - BEHIND) for j in range(BEHIND)]
    grad_own = add_parts(grad_kv[BEHIND], others)
    kv_rows = exchange(grad_own.reshape(sharers, rows, 2 * HEAD_SIZE))
    key_state_gradient, value_state_gradient = unpack_keys(kv_rows)
    return unpack_queries(grad_rows), key_state_gradient, value_state_gradient


def solution(mesh):
    split = P(("ctx", "head"), None)
    return jax.shard_map(
        on_device,
        mesh=mesh,
        in_specs=(split, split, split, split, split, P()),
        out_specs=(split, split, split),
        check_vma=False,
    )
```

```python
import math

import jax
import jax.numpy as jnp
from jax import lax
from jax.experimental import pallas as pl
from jax.experimental.pallas import tpu as pltpu
from jax.sharding import PartitionSpec as P

QUERY_HEAD_COUNT = 64
KEY_VALUE_HEADS = 8
HEAD_SIZE = 128
HEADS_EACH = QUERY_HEAD_COUNT // KEY_VALUE_HEADS
COLUMNS = HEADS_EACH * HEAD_SIZE
BEHIND = 4
SCALE = 1.0 / math.sqrt(HEAD_SIZE)
LOG2E = math.log2(math.e)
VMEM = pl.BlockSpec(memory_space=pltpu.VMEM)


def params(megabytes):
    return pltpu.CompilerParams(vmem_limit_bytes=megabytes * 1024 * 1024)


def contract_last(left, right):
    return lax.dot_general(
        left, right, (((1,), (1,)), ((), ())), preferred_element_type=jnp.float32
    )


def pack_keys(keys, values):
    rows = keys.shape[0]
    parts = [x.reshape(rows, KEY_VALUE_HEADS, HEAD_SIZE) for x in (keys, values)]
    return jnp.concatenate(parts, axis=-1).transpose(1, 0, 2)


def pack_queries_kernel(query_ref, out_ref, grad_ref, packed_ref):
    rows = query_ref.shape[0]
    lane = lax.broadcasted_iota(jnp.int32, (rows, HEAD_SIZE), 1)
    for c in range(KEY_VALUE_HEADS):
        columns = slice(c * COLUMNS, (c + 1) * COLUMNS)
        packed_ref[c, :, :COLUMNS] = query_ref[:, columns]
        packed_ref[c, :, COLUMNS : 2 * COLUMNS] = grad_ref[:, columns]
        terms = jnp.zeros((rows, HEAD_SIZE), jnp.float32)
        for h in range(HEADS_EACH):
            head = slice(c * COLUMNS + h * HEAD_SIZE, c * COLUMNS + (h + 1) * HEAD_SIZE)
            delta = jnp.sum(
                grad_ref[:, head].astype(jnp.float32) * out_ref[:, head].astype(jnp.float32),
                axis=-1,
                keepdims=True,
            )
            high = delta.astype(jnp.bfloat16).astype(jnp.float32)
            rest = delta - high
            middle = rest.astype(jnp.bfloat16).astype(jnp.float32)
            terms = jnp.where(lane == h, high, terms)
            terms = jnp.where(lane == HEADS_EACH + h, middle, terms)
            terms = jnp.where(lane == 2 * HEADS_EACH + h, rest - middle, terms)
        packed_ref[c, :, 2 * COLUMNS :] = terms.astype(jnp.bfloat16)


def pack_queries(queries, outputs, grads):
    rows = queries.shape[0]
    return pl.pallas_call(
        pack_queries_kernel,
        out_shape=jax.ShapeDtypeStruct(
            (KEY_VALUE_HEADS, rows, 2 * COLUMNS + HEAD_SIZE), jnp.bfloat16
        ),
        in_specs=[VMEM] * 3,
        out_specs=VMEM,
        name="pack_queries",
    )(queries, outputs, grads)


def attend_kernel(
    packed_ref, kv0, kv1, kv2, kv3, kv4, first_ref,
    grad_query_ref, out0, out1, out2, out3, out4,
    bias, key_turned, scores, delta, key_total, value_total,
):
    kv = (kv0, kv1, kv2, kv3, kv4)
    outs = (out0, out1, out2, out3, out4)
    block = kv0.shape[0]
    parts = len(kv)
    rows = [slice(j * block, (j + 1) * block) for j in range(parts)]
    first = first_ref[...]
    last = lax.broadcasted_iota(jnp.int32, (1, block), 1) + (parts - 1) * block
    for j in range(parts):
        key_at = lax.broadcasted_iota(jnp.int32, (block, block), 0) + j * block
        seen = (key_at >= first) & (key_at <= last)
        bias[rows[j], :] = jnp.where(seen, 0.0, -1e30)
        key_turned[:, rows[j]] = kv[j][:, :HEAD_SIZE].astype(jnp.float32).T.astype(jnp.bfloat16)
    terms = packed_ref[:, 2 * COLUMNS :].astype(jnp.float32).T
    delta[...] = (
        terms[:HEADS_EACH] + terms[HEADS_EACH : 2 * HEADS_EACH]
        + terms[2 * HEADS_EACH : 3 * HEADS_EACH]
    )
    key_total[...] = jnp.zeros_like(key_total)
    value_total[...] = jnp.zeros_like(value_total)

    sub = 256
    pieces = block * parts // sub
    spans = [slice(i * sub, (i + 1) * sub) for i in range(pieces)]
    group = 4
    wide = group * block
    def kvs(i, columns):
        j, o = divmod(i * sub, block)
        return kv[j][o : o + sub, columns]
    for g in range(HEADS_EACH // group):
        heads = range(g * group, (g + 1) * group)
        query = jnp.concatenate([packed_ref[:, h * HEAD_SIZE : (h + 1) * HEAD_SIZE] for h in heads], axis=0)
        grad = jnp.concatenate([packed_ref[:, COLUMNS + h * HEAD_SIZE : COLUMNS + (h + 1) * HEAD_SIZE] for h in heads], axis=0)
        row_delta = jnp.concatenate([delta[h : h + 1, :] for h in heads], axis=1)
        tops, sums = [], []
        for i in range(pieces):
            b = bias[spans[i], :]
            if group > 1:
                b = jnp.concatenate([b] * group, axis=1)
            part = contract_last(kvs(i, slice(0, HEAD_SIZE)), query) * (SCALE * LOG2E) + b
            top = jnp.max(part, axis=0, keepdims=True)
            part = jnp.exp2(part - top)
            scores[spans[i], :] = part.astype(scores.dtype)
            tops.append(top)
            sums.append(jnp.sum(part, axis=0, keepdims=True))
        largest = tops[0]
        for top in tops[1:]:
            largest = jnp.maximum(largest, top)
        factors = [jnp.exp2(top - largest) for top in tops]
        total = factors[0] * sums[0]
        for f, s in zip(factors[1:], sums[1:]):
            total = total + f * s
        inverse = 1.0 / total
        query_grad = jnp.zeros((HEAD_SIZE, wide), jnp.float32)
        for i in range(pieces):
            probs = scores[spans[i], :].astype(jnp.float32) * (factors[i] * inverse)
            value_total[spans[i], :] += jnp.dot(probs.astype(jnp.bfloat16), grad, preferred_element_type=jnp.float32)
            grad_probs = contract_last(kvs(i, slice(HEAD_SIZE, 2 * HEAD_SIZE)), grad)
            grad_scores = (probs * (grad_probs - row_delta)).astype(jnp.bfloat16)
            key_total[spans[i], :] += jnp.dot(grad_scores, query, preferred_element_type=jnp.float32)
            query_grad = query_grad + jnp.dot(key_turned[:, spans[i]], grad_scores, preferred_element_type=jnp.float32)
        for n, h in enumerate(heads):
            grad_query_ref[:, h * HEAD_SIZE : (h + 1) * HEAD_SIZE] = (query_grad[:, n * block : (n + 1) * block] * SCALE).T.astype(jnp.bfloat16)
    for j in range(parts):
        outs[j][:, :HEAD_SIZE] = (key_total[rows[j], :] * SCALE).astype(outs[j].dtype)
        outs[j][:, HEAD_SIZE:] = value_total[rows[j], :].astype(outs[j].dtype)


def attend(packed, kv, first):
    block = packed.shape[0]
    keys = block * len(kv)
    part = (block, 2 * HEAD_SIZE)
    return pl.pallas_call(
        attend_kernel,
        out_shape=[jax.ShapeDtypeStruct((block, COLUMNS), jnp.bfloat16)]
        + [jax.ShapeDtypeStruct(part, jnp.bfloat16)] * BEHIND
        + [jax.ShapeDtypeStruct(part, jnp.float32)],
        in_specs=[VMEM] * (2 + len(kv)),
        out_specs=[VMEM] * (1 + len(kv)),
        scratch_shapes=[
            pltpu.VMEM((keys, block), jnp.float32),
            pltpu.VMEM((HEAD_SIZE, keys), jnp.bfloat16),
            pltpu.VMEM((keys, 4 * block), jnp.float32),
            pltpu.VMEM((HEADS_EACH, block), jnp.float32),
            pltpu.VMEM((keys, HEAD_SIZE), jnp.float32),
            pltpu.VMEM((keys, HEAD_SIZE), jnp.float32),
        ],
        compiler_params=params(32),
        name="attend",
    )(packed, *kv, first)


def add_parts(own, others):
    for other in others:
        own = own + other.astype(jnp.float32)
    return own.astype(jnp.bfloat16)


def unpack_queries_kernel(in_ref, out_ref):
    for c in range(KEY_VALUE_HEADS):
        out_ref[:, c * COLUMNS : (c + 1) * COLUMNS] = in_ref[c]


def unpack_queries(packed):
    rows = packed.shape[1]
    return pl.pallas_call(
        unpack_queries_kernel,
        out_shape=jax.ShapeDtypeStruct((rows, KEY_VALUE_HEADS * COLUMNS), jnp.bfloat16),
        in_specs=[VMEM],
        out_specs=VMEM,
        name="unpack_queries",
    )(packed)


def unpack_keys(packed):
    rows = packed.shape[1]
    packed = packed.transpose(1, 0, 2)
    return tuple(
        packed[:, :, i * HEAD_SIZE : (i + 1) * HEAD_SIZE].reshape(rows, KEY_VALUE_HEADS * HEAD_SIZE)
        for i in range(2)
    )


def on_device(queries, key_state_rows, value_state_rows, attn_output, grad_output, doc_ids):
    placements = lax.axis_size("head")
    contexts = lax.axis_size("ctx")
    rows = queries.shape[0]
    sharers = KEY_VALUE_HEADS
    blocks_each = placements // sharers
    block = rows * sharers
    teams = [[t * sharers + i for i in range(sharers)] for t in range(blocks_each)]

    def exchange(value):
        return lax.all_to_all(
            value, "head", split_axis=0, concat_axis=0, axis_index_groups=teams, tiled=True
        )

    def shift(value, steps):
        count = contexts * blocks_each
        pairs = [
            (source * sharers + i, (source + steps) * sharers + i)
            for source in range(count)
            if 0 <= source + steps < count
            for i in range(sharers)
        ]
        return lax.ppermute(value, ("ctx", "head"), pairs)

    at = lax.axis_index("ctx") * blocks_each + lax.axis_index("head") // sharers
    padded = jnp.concatenate([jnp.full((BEHIND * block,), -1, jnp.int32), doc_ids])
    seg_key = lax.dynamic_slice_in_dim(padded, at * block, (BEHIND + 1) * block, 0)
    seg_query = seg_key[BEHIND * block :]
    first = jnp.sum((seg_key[:, None] < seg_query[None, :]).astype(jnp.int32), axis=0)[None, :]

    own = exchange(pack_keys(key_state_rows, value_state_rows)).reshape(block, 2 * HEAD_SIZE)
    packed = exchange(pack_queries(queries, attn_output, grad_output))
    packed = packed.reshape(block, 2 * COLUMNS + HEAD_SIZE)
    kv = [shift(own, steps) for steps in range(BEHIND, 0, -1)] + [own]
    grad_query, *grad_kv = attend(packed, kv, first)
    grad_rows = exchange(grad_query.reshape(sharers, rows, COLUMNS))
    others = [shift(grad_kv[j], j - BEHIND) for j in range(BEHIND)]
    grad_own = add_parts(grad_kv[BEHIND], others)
    grad_own, grad_rows = lax.optimization_barrier((grad_own, grad_rows))
    kv_rows = exchange(grad_own.reshape(sharers, rows, 2 * HEAD_SIZE))
    key_state_gradient, value_state_gradient = unpack_keys(kv_rows)
    return unpack_queries(grad_rows), key_state_gradient, value_state_gradient


def solution(mesh):
    split = P(("ctx", "head"), None)
    return jax.shard_map(
        on_device,
        mesh=mesh,
        in_specs=(split, split, split, split, split, P()),
        out_specs=(split, split, split),
        check_vma=False,
    )
```

```python
import math

import jax
import jax.numpy as jnp
from jax import lax
from jax.experimental import pallas as pl
from jax.experimental.pallas import tpu as pltpu
from jax.sharding import PartitionSpec as P

QUERY_HEAD_COUNT = 64
KEY_VALUE_HEADS = 8
HEAD_SIZE = 128
HEADS_EACH = QUERY_HEAD_COUNT // KEY_VALUE_HEADS
COLUMNS = HEADS_EACH * HEAD_SIZE
BEHIND = 4
SCALE = 1.0 / math.sqrt(HEAD_SIZE)
LOG2E = math.log2(math.e)
VMEM = pl.BlockSpec(memory_space=pltpu.VMEM)


def params(megabytes):
    return pltpu.CompilerParams(vmem_limit_bytes=megabytes * 1024 * 1024)


def contract_last(left, right):
    return lax.dot_general(
        left, right, (((1,), (1,)), ((), ())), preferred_element_type=jnp.float32
    )


def pack_keys_kernel(key_ref, value_ref, out_ref):
    for c in range(KEY_VALUE_HEADS):
        columns = slice(c * HEAD_SIZE, (c + 1) * HEAD_SIZE)
        out_ref[c, :, :HEAD_SIZE] = key_ref[:, columns]
        out_ref[c, :, HEAD_SIZE:] = value_ref[:, columns]


def pack_keys(keys, values):
    rows = keys.shape[0]
    return pl.pallas_call(
        pack_keys_kernel,
        out_shape=jax.ShapeDtypeStruct((KEY_VALUE_HEADS, rows, 2 * HEAD_SIZE), jnp.bfloat16),
        in_specs=[VMEM] * 2,
        out_specs=VMEM,
        name="pack_keys",
    )(keys, values)


def pack_queries_kernel(query_ref, out_ref, grad_ref, packed_ref):
    rows = query_ref.shape[0]
    lane = lax.broadcasted_iota(jnp.int32, (rows, HEAD_SIZE), 1)
    for c in range(KEY_VALUE_HEADS):
        columns = slice(c * COLUMNS, (c + 1) * COLUMNS)
        packed_ref[c, :, :COLUMNS] = query_ref[:, columns]
        packed_ref[c, :, COLUMNS : 2 * COLUMNS] = grad_ref[:, columns]
        terms = jnp.zeros((rows, HEAD_SIZE), jnp.float32)
        for h in range(HEADS_EACH):
            head = slice(c * COLUMNS + h * HEAD_SIZE, c * COLUMNS + (h + 1) * HEAD_SIZE)
            delta = jnp.sum(
                grad_ref[:, head].astype(jnp.float32) * out_ref[:, head].astype(jnp.float32),
                axis=-1,
                keepdims=True,
            )
            high = delta.astype(jnp.bfloat16).astype(jnp.float32)
            rest = delta - high
            middle = rest.astype(jnp.bfloat16).astype(jnp.float32)
            terms = jnp.where(lane == h, high, terms)
            terms = jnp.where(lane == HEADS_EACH + h, middle, terms)
            terms = jnp.where(lane == 2 * HEADS_EACH + h, rest - middle, terms)
        packed_ref[c, :, 2 * COLUMNS :] = terms.astype(jnp.bfloat16)


def pack_queries(queries, outputs, grads):
    rows = queries.shape[0]
    return pl.pallas_call(
        pack_queries_kernel,
        out_shape=jax.ShapeDtypeStruct(
            (KEY_VALUE_HEADS, rows, 2 * COLUMNS + HEAD_SIZE), jnp.bfloat16
        ),
        in_specs=[VMEM] * 3,
        out_specs=VMEM,
        name="pack_queries",
    )(queries, outputs, grads)


def attend_kernel(
    packed_ref, kv0, kv1, kv2, kv3, kv4, first_ref,
    grad_query_ref, out0, out1, out2, out3, out4,
    bias, keys_ref, values_ref, key_turned,
):
    kv = (kv0, kv1, kv2, kv3, kv4)
    outs = (out0, out1, out2, out3, out4)
    block = kv0.shape[0]
    parts = len(kv)
    heads = range(HEADS_EACH)
    rows = [slice(j * block, (j + 1) * block) for j in range(parts)]
    first = first_ref[...]
    last = lax.broadcasted_iota(jnp.int32, (1, block), 1) + (parts - 1) * block
    for j in range(parts):
        key_at = lax.broadcasted_iota(jnp.int32, (block, block), 0) + j * block
        seen = (key_at >= first) & (key_at <= last)
        bias[rows[j], :] = jnp.where(seen, 0.0, -1e30)
        keys = kv[j][:, :HEAD_SIZE]
        keys_ref[rows[j], :] = keys
        values_ref[rows[j], :] = kv[j][:, HEAD_SIZE:]
        key_turned[:, rows[j]] = keys.astype(jnp.float32).T.astype(jnp.bfloat16)
    terms = packed_ref[:, 2 * COLUMNS :].astype(jnp.float32).T
    delta = (
        terms[:HEADS_EACH] + terms[HEADS_EACH : 2 * HEADS_EACH]
        + terms[2 * HEADS_EACH : 3 * HEADS_EACH]
    )
    row_delta = jnp.concatenate([delta[h : h + 1] for h in heads], axis=1)

    def stacked(offset):
        columns = [offset + h * HEAD_SIZE for h in heads]
        return jnp.concatenate([packed_ref[:, c : c + HEAD_SIZE] for c in columns], axis=0)

    query, grad = stacked(0), stacked(COLUMNS)
    masks = jnp.concatenate([bias[...]] * HEADS_EACH, axis=1)
    probs = contract_last(keys_ref[...], query) * (SCALE * LOG2E) + masks
    probs = jnp.exp2(probs - jnp.max(probs, axis=0, keepdims=True))
    probs = probs * (1.0 / jnp.sum(probs, axis=0, keepdims=True))
    value_grad = jnp.dot(probs.astype(jnp.bfloat16), grad, preferred_element_type=jnp.float32)
    grad_probs = contract_last(values_ref[...], grad)
    grad_scores = (probs * (grad_probs - row_delta)).astype(jnp.bfloat16)
    key_grad = jnp.dot(grad_scores, query, preferred_element_type=jnp.float32) * SCALE
    query_grad = jnp.dot(key_turned[...], grad_scores, preferred_element_type=jnp.float32) * SCALE
    for h in heads:
        part = query_grad[:, h * block : (h + 1) * block]
        grad_query_ref[:, h * HEAD_SIZE : (h + 1) * HEAD_SIZE] = part.T.astype(jnp.bfloat16)
    for j in range(parts):
        outs[j][:, :HEAD_SIZE] = key_grad[rows[j], :].astype(outs[j].dtype)
        outs[j][:, HEAD_SIZE:] = value_grad[rows[j], :].astype(outs[j].dtype)


def attend(packed, kv, first):
    block = packed.shape[0]
    keys = block * len(kv)
    part = (block, 2 * HEAD_SIZE)
    return pl.pallas_call(
        attend_kernel,
        out_shape=[jax.ShapeDtypeStruct((block, COLUMNS), jnp.bfloat16)]
        + [jax.ShapeDtypeStruct(part, jnp.bfloat16)] * BEHIND
        + [jax.ShapeDtypeStruct(part, jnp.float32)],
        in_specs=[VMEM] * (2 + len(kv)),
        out_specs=[VMEM] * (1 + len(kv)),
        scratch_shapes=[
            pltpu.VMEM((keys, block), jnp.float32),
            pltpu.VMEM((keys, HEAD_SIZE), jnp.bfloat16),
            pltpu.VMEM((keys, HEAD_SIZE), jnp.bfloat16),
            pltpu.VMEM((HEAD_SIZE, keys), jnp.bfloat16),
        ],
        compiler_params=params(50),
        name="attend",
    )(packed, *kv, first)


def add_parts(own, others):
    for other in others:
        own = own + other.astype(jnp.float32)
    return own.astype(jnp.bfloat16)


def unpack_queries_kernel(in_ref, out_ref):
    for c in range(KEY_VALUE_HEADS):
        out_ref[:, c * COLUMNS : (c + 1) * COLUMNS] = in_ref[c]


def unpack_queries(packed):
    rows = packed.shape[1]
    return pl.pallas_call(
        unpack_queries_kernel,
        out_shape=jax.ShapeDtypeStruct((rows, KEY_VALUE_HEADS * COLUMNS), jnp.bfloat16),
        in_specs=[VMEM],
        out_specs=VMEM,
        name="unpack_queries",
    )(packed)


def unpack_keys(packed):
    rows = packed.shape[1]
    packed = packed.transpose(1, 0, 2)
    return tuple(
        packed[:, :, i * HEAD_SIZE : (i + 1) * HEAD_SIZE].reshape(rows, KEY_VALUE_HEADS * HEAD_SIZE)
        for i in range(2)
    )


def on_device(queries, key_state_rows, value_state_rows, attn_output, grad_output, doc_ids):
    placements = lax.axis_size("head")
    contexts = lax.axis_size("ctx")
    rows = queries.shape[0]
    sharers = KEY_VALUE_HEADS
    blocks_each = placements // sharers
    block = rows * sharers
    teams = [[t * sharers + i for i in range(sharers)] for t in range(blocks_each)]

    def exchange(value):
        return lax.all_to_all(
            value, "head", split_axis=0, concat_axis=0, axis_index_groups=teams, tiled=True
        )

    def shift(value, steps):
        count = contexts * blocks_each
        pairs = [
            (source * sharers + i, (source + steps) * sharers + i)
            for source in range(count)
            if 0 <= source + steps < count
            for i in range(sharers)
        ]
        return lax.ppermute(value, ("ctx", "head"), pairs)

    at = lax.axis_index("ctx") * blocks_each + lax.axis_index("head") // sharers
    padded = jnp.concatenate([jnp.full((BEHIND * block,), -1, jnp.int32), doc_ids])
    seg_key = lax.dynamic_slice_in_dim(padded, at * block, (BEHIND + 1) * block, 0)
    seg_query = seg_key[BEHIND * block :]
    first = jnp.sum((seg_key[:, None] < seg_query[None, :]).astype(jnp.int32), axis=0)[None, :]

    own = exchange(pack_keys(key_state_rows, value_state_rows)).reshape(block, 2 * HEAD_SIZE)
    packed = exchange(pack_queries(queries, attn_output, grad_output))
    packed = packed.reshape(block, 2 * COLUMNS + HEAD_SIZE)
    kv = [shift(own, steps) for steps in range(BEHIND, 0, -1)] + [own]
    grad_query, *grad_kv = attend(packed, kv, first)
    grad_rows = exchange(grad_query.reshape(sharers, rows, COLUMNS))
    others = [shift(grad_kv[j], j - BEHIND) for j in range(BEHIND)]
    grad_own = add_parts(grad_kv[BEHIND], others)
    grad_own, grad_rows = lax.optimization_barrier((grad_own, grad_rows))
    kv_rows = exchange(grad_own.reshape(sharers, rows, 2 * HEAD_SIZE))
    key_state_gradient, value_state_gradient = unpack_keys(kv_rows)
    return unpack_queries(grad_rows), key_state_gradient, value_state_gradient


def solution(mesh):
    split = P(("ctx", "head"), None)
    return jax.shard_map(
        on_device,
        mesh=mesh,
        in_specs=(split, split, split, split, split, P()),
        out_specs=(split, split, split),
        check_vma=False,
    )
```

```python
import math

import jax
import jax.numpy as jnp
from jax import lax
from jax.experimental import pallas as pl
from jax.experimental.pallas import tpu as pltpu
from jax.sharding import PartitionSpec as P

QUERY_HEAD_COUNT = 64
KEY_VALUE_HEADS = 8
HEAD_SIZE = 128
HEADS_EACH = QUERY_HEAD_COUNT // KEY_VALUE_HEADS
COLUMNS = HEADS_EACH * HEAD_SIZE
BEHIND = 4
SCALE = 1.0 / math.sqrt(HEAD_SIZE)
LOG2E = math.log2(math.e)
VMEM = pl.BlockSpec(memory_space=pltpu.VMEM)


def params(megabytes):
    return pltpu.CompilerParams(vmem_limit_bytes=megabytes * 1024 * 1024)


def contract_last(left, right):
    return lax.dot_general(
        left, right, (((1,), (1,)), ((), ())), preferred_element_type=jnp.float32
    )


def pack_keys_kernel(key_ref, value_ref, out_ref):
    for c in range(KEY_VALUE_HEADS):
        columns = slice(c * HEAD_SIZE, (c + 1) * HEAD_SIZE)
        out_ref[c, :, :HEAD_SIZE] = key_ref[:, columns]
        out_ref[c, :, HEAD_SIZE:] = value_ref[:, columns]


def pack_keys(keys, values):
    rows = keys.shape[0]
    return pl.pallas_call(
        pack_keys_kernel,
        out_shape=jax.ShapeDtypeStruct((KEY_VALUE_HEADS, rows, 2 * HEAD_SIZE), jnp.bfloat16),
        in_specs=[VMEM] * 2,
        out_specs=VMEM,
        name="pack_keys",
    )(keys, values)


def pack_queries_kernel(query_ref, out_ref, grad_ref, packed_ref):
    rows = query_ref.shape[0]
    lane = lax.broadcasted_iota(jnp.int32, (rows, HEAD_SIZE), 1)
    for c in range(KEY_VALUE_HEADS):
        columns = slice(c * COLUMNS, (c + 1) * COLUMNS)
        packed_ref[c, :, :COLUMNS] = query_ref[:, columns]
        packed_ref[c, :, COLUMNS : 2 * COLUMNS] = grad_ref[:, columns]
        terms = jnp.zeros((rows, HEAD_SIZE), jnp.float32)
        for h in range(HEADS_EACH):
            head = slice(c * COLUMNS + h * HEAD_SIZE, c * COLUMNS + (h + 1) * HEAD_SIZE)
            delta = jnp.sum(
                grad_ref[:, head].astype(jnp.float32) * out_ref[:, head].astype(jnp.float32),
                axis=-1,
                keepdims=True,
            )
            high = delta.astype(jnp.bfloat16).astype(jnp.float32)
            rest = delta - high
            middle = rest.astype(jnp.bfloat16).astype(jnp.float32)
            terms = jnp.where(lane == h, high, terms)
            terms = jnp.where(lane == HEADS_EACH + h, middle, terms)
            terms = jnp.where(lane == 2 * HEADS_EACH + h, rest - middle, terms)
        packed_ref[c, :, 2 * COLUMNS :] = terms.astype(jnp.bfloat16)


def pack_queries(queries, outputs, grads):
    rows = queries.shape[0]
    return pl.pallas_call(
        pack_queries_kernel,
        out_shape=jax.ShapeDtypeStruct(
            (KEY_VALUE_HEADS, rows, 2 * COLUMNS + HEAD_SIZE), jnp.bfloat16
        ),
        in_specs=[VMEM] * 3,
        out_specs=VMEM,
        name="pack_queries",
    )(queries, outputs, grads)


def attend_kernel(
    packed_ref, kv0, kv1, kv2, kv3, kv4, first_ref,
    grad_query_ref, out0, out1, out2, out3, out4,
    bias, keys_ref, values_ref, key_turned, key_total, value_total,
):
    kv = (kv0, kv1, kv2, kv3, kv4)
    outs = (out0, out1, out2, out3, out4)
    block = kv0.shape[0]
    parts = len(kv)
    heads = range(HEADS_EACH)
    rows = [slice(j * block, (j + 1) * block) for j in range(parts)]
    first = first_ref[...]
    last = lax.broadcasted_iota(jnp.int32, (1, block), 1) + (parts - 1) * block
    for j in range(parts):
        key_at = lax.broadcasted_iota(jnp.int32, (block, block), 0) + j * block
        seen = (key_at >= first) & (key_at <= last)
        bias[rows[j], :] = jnp.where(seen, 0.0, -1e30)
        keys = kv[j][:, :HEAD_SIZE]
        keys_ref[rows[j], :] = keys
        values_ref[rows[j], :] = kv[j][:, HEAD_SIZE:]
        key_turned[:, rows[j]] = keys.astype(jnp.float32).T.astype(jnp.bfloat16)
    terms = packed_ref[:, 2 * COLUMNS :].astype(jnp.float32).T
    delta = (
        terms[:HEADS_EACH] + terms[HEADS_EACH : 2 * HEADS_EACH]
        + terms[2 * HEADS_EACH : 3 * HEADS_EACH]
    )
    step = block // 2
    reach = (parts - 1) * block + step

    def weigh(part):
        token = slice(part * step, (part + 1) * step)
        near = slice(part * step, part * step + reach)

        def stacked(offset):
            columns = [offset + h * HEAD_SIZE for h in heads]
            return jnp.concatenate([packed_ref[token, c : c + HEAD_SIZE] for c in columns], axis=0)

        query, grad = stacked(0), stacked(COLUMNS)
        masks = jnp.concatenate([bias[near, token]] * HEADS_EACH, axis=1)
        raw = contract_last(keys_ref[near, :], query) * (SCALE * LOG2E) + masks
        return query, grad, raw, jnp.max(raw, axis=0, keepdims=True)

    def normalize(part, query, grad, raw, largest):
        near = slice(part * step, part * step + reach)
        weights = jnp.exp2(raw - largest)
        inverse = 1.0 / jnp.sum(weights, axis=0, keepdims=True)
        return query, grad, weights, inverse, contract_last(values_ref[near, :], grad)

    def finish(part, query, grad, weights, inverse, grad_probs):
        token = slice(part * step, (part + 1) * step)
        near = slice(part * step, part * step + reach)
        row_delta = jnp.concatenate([delta[h : h + 1, token] for h in heads], axis=1)
        probs = weights * inverse
        grad_scores = (probs * (grad_probs - row_delta)).astype(jnp.bfloat16)
        value_grad = jnp.dot(probs.astype(jnp.bfloat16), grad, preferred_element_type=jnp.float32)
        key_grad = jnp.dot(grad_scores, query, preferred_element_type=jnp.float32)
        query_grad = (
            jnp.dot(key_turned[:, near], grad_scores, preferred_element_type=jnp.float32) * SCALE
        )
        for h in heads:
            turned = query_grad[:, h * step : (h + 1) * step].T.astype(jnp.bfloat16)
            grad_query_ref[token, h * HEAD_SIZE : (h + 1) * HEAD_SIZE] = turned
        if part == 0:
            key_total[near, :] = key_grad
            value_total[near, :] = value_grad
        else:
            both, new = slice(near.start, reach), slice(reach, near.stop)
            key_total[both, :] += key_grad[: reach - step]
            value_total[both, :] += value_grad[: reach - step]
            key_total[new, :] = key_grad[reach - step :]
            value_total[new, :] = value_grad[reach - step :]

    weighed = [weigh(part) for part in range(2)]
    normal = [normalize(part, *weighed[part]) for part in range(2)]
    for part in range(2):
        finish(part, *normal[part])
    for j in range(parts):
        outs[j][:, :HEAD_SIZE] = (key_total[rows[j], :] * SCALE).astype(outs[j].dtype)
        outs[j][:, HEAD_SIZE:] = value_total[rows[j], :].astype(outs[j].dtype)


def attend(packed, kv, first):
    block = packed.shape[0]
    keys = block * len(kv)
    part = (block, 2 * HEAD_SIZE)
    return pl.pallas_call(
        attend_kernel,
        out_shape=[jax.ShapeDtypeStruct((block, COLUMNS), jnp.bfloat16)]
        + [jax.ShapeDtypeStruct(part, jnp.bfloat16)] * BEHIND
        + [jax.ShapeDtypeStruct(part, jnp.float32)],
        in_specs=[VMEM] * (2 + len(kv)),
        out_specs=[VMEM] * (1 + len(kv)),
        scratch_shapes=[
            pltpu.VMEM((keys, block), jnp.float32),
            pltpu.VMEM((keys, HEAD_SIZE), jnp.bfloat16),
            pltpu.VMEM((keys, HEAD_SIZE), jnp.bfloat16),
            pltpu.VMEM((HEAD_SIZE, keys), jnp.bfloat16),
            pltpu.VMEM((keys, HEAD_SIZE), jnp.float32),
            pltpu.VMEM((keys, HEAD_SIZE), jnp.float32),
        ],
        compiler_params=params(50),
        name="attend",
    )(packed, *kv, first)


def add_parts(own, others):
    for other in others:
        own = own + other.astype(jnp.float32)
    return own.astype(jnp.bfloat16)


def unpack_queries_kernel(in_ref, out_ref):
    for c in range(KEY_VALUE_HEADS):
        out_ref[:, c * COLUMNS : (c + 1) * COLUMNS] = in_ref[c]


def unpack_queries(packed):
    rows = packed.shape[1]
    return pl.pallas_call(
        unpack_queries_kernel,
        out_shape=jax.ShapeDtypeStruct((rows, KEY_VALUE_HEADS * COLUMNS), jnp.bfloat16),
        in_specs=[VMEM],
        out_specs=VMEM,
        name="unpack_queries",
    )(packed)


def unpack_keys(packed):
    rows = packed.shape[1]
    packed = packed.transpose(1, 0, 2)
    return tuple(
        packed[:, :, i * HEAD_SIZE : (i + 1) * HEAD_SIZE].reshape(rows, KEY_VALUE_HEADS * HEAD_SIZE)
        for i in range(2)
    )


def on_device(queries, key_state_rows, value_state_rows, attn_output, grad_output, doc_ids):
    placements = lax.axis_size("head")
    contexts = lax.axis_size("ctx")
    rows = queries.shape[0]
    sharers = KEY_VALUE_HEADS
    blocks_each = placements // sharers
    block = rows * sharers
    teams = [[t * sharers + i for i in range(sharers)] for t in range(blocks_each)]

    def exchange(value):
        return lax.all_to_all(
            value, "head", split_axis=0, concat_axis=0, axis_index_groups=teams, tiled=True
        )

    def shift(value, steps):
        count = contexts * blocks_each
        pairs = [
            (source * sharers + i, (source + steps) * sharers + i)
            for source in range(count)
            if 0 <= source + steps < count
            for i in range(sharers)
        ]
        return lax.ppermute(value, ("ctx", "head"), pairs)

    at = lax.axis_index("ctx") * blocks_each + lax.axis_index("head") // sharers
    padded = jnp.concatenate([jnp.full((BEHIND * block,), -1, jnp.int32), doc_ids])
    seg_key = lax.dynamic_slice_in_dim(padded, at * block, (BEHIND + 1) * block, 0)
    seg_query = seg_key[BEHIND * block :]
    first = jnp.sum((seg_key[:, None] < seg_query[None, :]).astype(jnp.int32), axis=0)[None, :]

    own = exchange(pack_keys(key_state_rows, value_state_rows)).reshape(block, 2 * HEAD_SIZE)
    packed = exchange(pack_queries(queries, attn_output, grad_output))
    packed = packed.reshape(block, 2 * COLUMNS + HEAD_SIZE)
    kv = [shift(own, steps) for steps in range(BEHIND, 0, -1)] + [own]
    grad_query, *grad_kv = attend(packed, kv, first)
    grad_rows = exchange(grad_query.reshape(sharers, rows, COLUMNS))
    others = [shift(grad_kv[j], j - BEHIND) for j in range(BEHIND)]
    grad_own = add_parts(grad_kv[BEHIND], others)
    grad_own, grad_rows = lax.optimization_barrier((grad_own, grad_rows))
    kv_rows = exchange(grad_own.reshape(sharers, rows, 2 * HEAD_SIZE))
    key_state_gradient, value_state_gradient = unpack_keys(kv_rows)
    return unpack_queries(grad_rows), key_state_gradient, value_state_gradient


def solution(mesh):
    split = P(("ctx", "head"), None)
    return jax.shard_map(
        on_device,
        mesh=mesh,
        in_specs=(split, split, split, split, split, P()),
        out_specs=(split, split, split),
        check_vma=False,
    )
```

```python
import math

import jax
import jax.numpy as jnp
from jax import lax
from jax.experimental import pallas as pl
from jax.experimental.pallas import tpu as pltpu
from jax.sharding import PartitionSpec as P

QUERY_HEAD_COUNT = 64
KEY_VALUE_HEADS = 8
HEAD_SIZE = 128
HEADS_EACH = QUERY_HEAD_COUNT // KEY_VALUE_HEADS
COLUMNS = HEADS_EACH * HEAD_SIZE
BEHIND = 4
SCALE = 1.0 / math.sqrt(HEAD_SIZE)
LOG2E = math.log2(math.e)
VMEM = pl.BlockSpec(memory_space=pltpu.VMEM)


def params(megabytes):
    return pltpu.CompilerParams(vmem_limit_bytes=megabytes * 1024 * 1024)


def contract_last(left, right):
    return lax.dot_general(
        left, right, (((1,), (1,)), ((), ())), preferred_element_type=jnp.float32
    )


def pack_keys_kernel(key_ref, value_ref, out_ref):
    for c in range(KEY_VALUE_HEADS):
        columns = slice(c * HEAD_SIZE, (c + 1) * HEAD_SIZE)
        out_ref[c, :, :HEAD_SIZE] = key_ref[:, columns]
        out_ref[c, :, HEAD_SIZE:] = value_ref[:, columns]


def pack_keys(keys, values):
    rows = keys.shape[0]
    return pl.pallas_call(
        pack_keys_kernel,
        out_shape=jax.ShapeDtypeStruct((KEY_VALUE_HEADS, rows, 2 * HEAD_SIZE), jnp.bfloat16),
        in_specs=[VMEM] * 2,
        out_specs=VMEM,
        name="pack_keys",
    )(keys, values)


def pack_queries_kernel(query_ref, out_ref, grad_ref, packed_ref):
    rows = query_ref.shape[0]
    lane = lax.broadcasted_iota(jnp.int32, (rows, HEAD_SIZE), 1)
    for c in range(KEY_VALUE_HEADS):
        columns = slice(c * COLUMNS, (c + 1) * COLUMNS)
        packed_ref[c, :, :COLUMNS] = query_ref[:, columns]
        packed_ref[c, :, COLUMNS : 2 * COLUMNS] = grad_ref[:, columns]
        terms = jnp.zeros((rows, HEAD_SIZE), jnp.float32)
        for h in range(HEADS_EACH):
            head = slice(c * COLUMNS + h * HEAD_SIZE, c * COLUMNS + (h + 1) * HEAD_SIZE)
            delta = jnp.sum(
                grad_ref[:, head].astype(jnp.float32) * out_ref[:, head].astype(jnp.float32),
                axis=-1,
                keepdims=True,
            )
            high = delta.astype(jnp.bfloat16).astype(jnp.float32)
            rest = delta - high
            middle = rest.astype(jnp.bfloat16).astype(jnp.float32)
            terms = jnp.where(lane == h, high, terms)
            terms = jnp.where(lane == HEADS_EACH + h, middle, terms)
            terms = jnp.where(lane == 2 * HEADS_EACH + h, rest - middle, terms)
        packed_ref[c, :, 2 * COLUMNS :] = terms.astype(jnp.bfloat16)


def pack_queries(queries, outputs, grads):
    rows = queries.shape[0]
    return pl.pallas_call(
        pack_queries_kernel,
        out_shape=jax.ShapeDtypeStruct(
            (KEY_VALUE_HEADS, rows, 2 * COLUMNS + HEAD_SIZE), jnp.bfloat16
        ),
        in_specs=[VMEM] * 3,
        out_specs=VMEM,
        name="pack_queries",
    )(queries, outputs, grads)


def attend_kernel(
    packed_ref, kv0, kv1, kv2, kv3, kv4, first_ref,
    grad_query_ref, out0, out1, out2, out3, out4,
    bias, keys_ref, values_ref, key_turned, key_total, value_total,
):
    kv = (kv0, kv1, kv2, kv3, kv4)
    outs = (out0, out1, out2, out3, out4)
    block = kv0.shape[0]
    parts = len(kv)
    heads = range(HEADS_EACH)
    rows = [slice(j * block, (j + 1) * block) for j in range(parts)]
    first = first_ref[...]
    last = lax.broadcasted_iota(jnp.int32, (1, block), 1) + (parts - 1) * block
    for j in range(parts):
        key_at = lax.broadcasted_iota(jnp.int32, (block, block), 0) + j * block
        seen = (key_at >= first) & (key_at <= last)
        bias[rows[j], :] = jnp.where(seen, 0.0, -1e30)
        keys = kv[j][:, :HEAD_SIZE]
        keys_ref[rows[j], :] = keys
        values_ref[rows[j], :] = kv[j][:, HEAD_SIZE:]
        key_turned[:, rows[j]] = keys.astype(jnp.float32).T.astype(jnp.bfloat16)
    terms = packed_ref[:, 2 * COLUMNS :].astype(jnp.float32).T
    delta = (
        terms[:HEADS_EACH] + terms[HEADS_EACH : 2 * HEADS_EACH]
        + terms[2 * HEADS_EACH : 3 * HEADS_EACH]
    )
    step = block // 2
    reach = (parts - 1) * block + step

    def weigh(part):
        token = slice(part * step, (part + 1) * step)
        near = slice(part * step, part * step + reach)

        def stacked(offset):
            columns = [offset + h * HEAD_SIZE for h in heads]
            return jnp.concatenate([packed_ref[token, c : c + HEAD_SIZE] for c in columns], axis=0)

        query, grad = stacked(0), stacked(COLUMNS)
        masks = jnp.concatenate([bias[near, token]] * HEADS_EACH, axis=1)
        raw = contract_last(keys_ref[near, :], query) * (SCALE * LOG2E) + masks
        return query, grad, raw, jnp.max(raw, axis=0, keepdims=True)

    def normalize(part, query, grad, raw, largest):
        near = slice(part * step, part * step + reach)
        weights = jnp.exp2(raw - largest)
        inverse = 1.0 / jnp.sum(weights, axis=0, keepdims=True)
        return query, grad, weights, inverse, contract_last(values_ref[near, :], grad)

    def finish(part, query, grad, weights, inverse, grad_probs):
        token = slice(part * step, (part + 1) * step)
        near = slice(part * step, part * step + reach)
        row_delta = jnp.concatenate([delta[h : h + 1, token] for h in heads], axis=1)
        probs = weights * inverse
        grad_scores = (probs * (grad_probs - row_delta)).astype(jnp.bfloat16)
        value_grad = jnp.dot(probs.astype(jnp.bfloat16), grad, preferred_element_type=jnp.float32)
        key_grad = jnp.dot(grad_scores, query, preferred_element_type=jnp.float32)
        query_grad = (
            jnp.dot(key_turned[:, near], grad_scores, preferred_element_type=jnp.float32) * SCALE
        )
        for h in heads:
            turned = query_grad[:, h * step : (h + 1) * step].T.astype(jnp.bfloat16)
            grad_query_ref[token, h * HEAD_SIZE : (h + 1) * HEAD_SIZE] = turned
        if part == 0:
            key_total[near, :] = key_grad
            value_total[near, :] = value_grad
        else:
            both, new = slice(near.start, reach), slice(reach, near.stop)
            key_total[both, :] += key_grad[: reach - step]
            value_total[both, :] += value_grad[: reach - step]
            key_total[new, :] = key_grad[reach - step :]
            value_total[new, :] = value_grad[reach - step :]

    weighed = [weigh(part) for part in range(2)]
    normal = [normalize(part, *weighed[part]) for part in range(2)]
    for part in range(2):
        finish(part, *normal[part])
    for j in range(parts):
        outs[j][:, :HEAD_SIZE] = (key_total[rows[j], :] * SCALE).astype(outs[j].dtype)
        outs[j][:, HEAD_SIZE:] = value_total[rows[j], :].astype(outs[j].dtype)


def attend(packed, kv, first):
    block = packed.shape[0]
    keys = block * len(kv)
    part = (block, 2 * HEAD_SIZE)
    return pl.pallas_call(
        attend_kernel,
        out_shape=[jax.ShapeDtypeStruct((block, COLUMNS), jnp.bfloat16)]
        + [jax.ShapeDtypeStruct(part, jnp.bfloat16)] * BEHIND
        + [jax.ShapeDtypeStruct(part, jnp.float32)],
        in_specs=[VMEM] * (2 + len(kv)),
        out_specs=[VMEM] * (1 + len(kv)),
        scratch_shapes=[
            pltpu.VMEM((keys, block), jnp.float32),
            pltpu.VMEM((keys, HEAD_SIZE), jnp.bfloat16),
            pltpu.VMEM((keys, HEAD_SIZE), jnp.bfloat16),
            pltpu.VMEM((HEAD_SIZE, keys), jnp.bfloat16),
            pltpu.VMEM((keys, HEAD_SIZE), jnp.float32),
            pltpu.VMEM((keys, HEAD_SIZE), jnp.float32),
        ],
        compiler_params=params(50),
        name="attend",
    )(packed, *kv, first)


def add_parts(own, others):
    for other in others:
        own = own + other.astype(jnp.float32)
    return own.astype(jnp.bfloat16)


def unpack_queries_kernel(in_ref, out_ref):
    for c in range(KEY_VALUE_HEADS):
        out_ref[:, c * COLUMNS : (c + 1) * COLUMNS] = in_ref[c]


def unpack_queries(packed):
    rows = packed.shape[1]
    return pl.pallas_call(
        unpack_queries_kernel,
        out_shape=jax.ShapeDtypeStruct((rows, KEY_VALUE_HEADS * COLUMNS), jnp.bfloat16),
        in_specs=[VMEM],
        out_specs=VMEM,
        name="unpack_queries",
    )(packed)


def unpack_keys(packed):
    rows = packed.shape[1]
    packed = packed.transpose(1, 0, 2)
    return tuple(
        packed[:, :, i * HEAD_SIZE : (i + 1) * HEAD_SIZE].reshape(rows, KEY_VALUE_HEADS * HEAD_SIZE)
        for i in range(2)
    )


def on_device(queries, key_state_rows, value_state_rows, attn_output, grad_output, doc_ids):
    placements = lax.axis_size("head")
    contexts = lax.axis_size("ctx")
    rows = queries.shape[0]
    sharers = KEY_VALUE_HEADS
    blocks_each = placements // sharers
    block = rows * sharers
    teams = [[t * sharers + i for i in range(sharers)] for t in range(blocks_each)]

    def exchange(value):
        return lax.all_to_all(
            value, "head", split_axis=0, concat_axis=0, axis_index_groups=teams, tiled=True
        )

    def shift(value, steps):
        count = contexts * blocks_each
        pairs = [
            (source * sharers + i, (source + steps) * sharers + i)
            for source in range(count)
            if 0 <= source + steps < count
            for i in range(sharers)
        ]
        return lax.ppermute(value, ("ctx", "head"), pairs)

    at = lax.axis_index("ctx") * blocks_each + lax.axis_index("head") // sharers
    padded = jnp.concatenate([jnp.full((BEHIND * block,), -1, jnp.int32), doc_ids])
    seg_key = lax.dynamic_slice_in_dim(padded, at * block, (BEHIND + 1) * block, 0)
    seg_query = seg_key[BEHIND * block :]
    first = jnp.sum((seg_key[:, None] < seg_query[None, :]).astype(jnp.int32), axis=0)[None, :]

    own = exchange(pack_keys(key_state_rows, value_state_rows)).reshape(block, 2 * HEAD_SIZE)
    packed = exchange(pack_queries(queries, attn_output, grad_output))
    packed = packed.reshape(block, 2 * COLUMNS + HEAD_SIZE)
    kv = [shift(own, steps) for steps in range(BEHIND, 0, -1)] + [own]
    grad_query, *grad_kv = attend(packed, kv, first)
    grad_rows = exchange(grad_query.reshape(sharers, rows, COLUMNS))
    others = [shift(grad_kv[BEHIND - steps], -steps) for steps in (3, 2, 4, 1)]
    grad_own = add_parts(grad_kv[BEHIND], others)
    grad_own, grad_rows = lax.optimization_barrier((grad_own, grad_rows))
    kv_rows = exchange(grad_own.reshape(sharers, rows, 2 * HEAD_SIZE))
    key_state_gradient, value_state_gradient = unpack_keys(kv_rows)
    return unpack_queries(grad_rows), key_state_gradient, value_state_gradient


def solution(mesh):
    split = P(("ctx", "head"), None)
    return jax.shard_map(
        on_device,
        mesh=mesh,
        in_specs=(split, split, split, split, split, P()),
        out_specs=(split, split, split),
        check_vma=False,
    )
```
